32 devices in a mesh: sec: 4 (over y, x), mpo: 8 (over z, core).
Axes of the slice: x: 2, y: 2, z: 4, core: 2. Of those that a mesh axis runs over, the one named last changes fastest.
Arguments:
- wavefunction: bfloat16 [64, 128, 128], P('sec')
- left_size: int32 [64], P('sec'), may hold values from 32 to 128, as said below
- right_size: int32 [64], replicated, may hold values from 32 to 128, as said below
- right_sector: int32 [64], replicated, may hold values from 0 to 63, as said below
- left_environment: bfloat16 [16, 64, 128, 128], P('mpo', 'sec')
- right_environment: bfloat16 [16, 64, 128, 128], P('mpo', 'sec')
- term_weights: float32 [16], P('mpo'), may hold values from -0.4 to 0.4
Outputs:
- next_vector: float32 [64, 128, 128], P('sec', 'mpo')
- residual: float32 [64, 128, 128], P('sec', 'mpo')
- coefficients: float32 [3], replicated
The draws below stay inside these ranges and needn't reach their ends.
Inputs may be any that keep to these rules, and one draw needn't show every extreme that they name: `left_size`: some left sector has all 128 rows live. `right_size`: some right sector has all 128 columns live. `right_sector`: a permutation of the 64 sectors; of the left sectors of one index of sec (16 in a row) at most 6 pair with right sectors of any one index of sec (also 16 in a row), and some such pair of indices has exactly 6.
All inputs are finite; a program needn't handle non-finite values.
Results may differ from the reference program's by a relative error of at most 0.0064.
Values may be sent and summed in bfloat16 or wider, within the bound.
A program may use at most 64 MiB of HBM per device.

```python
import math
import jax
import jax.numpy as jnp
from jax import lax

B = 128
SEC_DEV = 16
NSEC = 64
WT = 16


def scaled_field(key_noise, key_rows, key_cols, log_top):
    base_values = jax.random.normal(key_noise, (NSEC, B, B), jnp.float32)
    row_scale = jnp.exp(jax.random.uniform(key_rows, (NSEC, B, 1), jnp.float32, 0.0, log_top))
    col_scale = jnp.exp(jax.random.uniform(key_cols, (NSEC, 1, B), jnp.float32, 0.0, log_top))
    rising = 1.0 + 2.0 * jnp.arange(NSEC, dtype=jnp.float32) / max(NSEC - 1, 1)
    return base_values * row_scale * col_scale * rising[:, None, None] / 10.0


def draw_wavefunction(key, part):
    key = jax.random.fold_in(key, 11)
    key_noise, key_rows, key_cols = jax.random.split(key, 3)
    return scaled_field(key_noise, key_rows, key_cols, 2.3).astype(jnp.bfloat16)


def sector_sizes(key):
    key_sizes, key_full = jax.random.split(key)
    drawn_size = jax.random.randint(key_sizes, (NSEC,), B // 4, B + 1)
    full_index = jax.random.randint(key_full, (), 0, NSEC)
    return jnp.where(jnp.arange(NSEC) == full_index, B, drawn_size).astype(jnp.int32)


def draw_left_size(key, part):
    key = jax.random.fold_in(key, 23)
    return sector_sizes(key)


def draw_right_size(key, part):
    key = jax.random.fold_in(key, 29)
    return sector_sizes(key)


def draw_right_sector(key, part):
    key = jax.random.fold_in(key, 41)
    key_spread, key_offset, key_shuffle, key_order = jax.random.split(key, 4)
    devices = NSEC // SEC_DEV
    average = SEC_DEV // devices
    surplus = max(1, average // 2)
    base_values = jnp.zeros((devices,), jnp.int32).at[0].set(surplus).at[1].set(-surplus)
    spread = jax.random.permutation(key_spread, base_values)
    offset = jax.random.randint(key_offset, (), 0, devices)
    source_ids = jnp.arange(devices, dtype=jnp.int32)[:, None]
    target_ids = jnp.arange(devices, dtype=jnp.int32)[None, :]
    counts = average + spread[(target_ids - source_ids + offset) % devices]
    limits = jnp.cumsum(counts, axis=1)
    slot_ids = jnp.arange(SEC_DEV, dtype=jnp.int32)
    dest_sorted = jnp.sum((limits[:, None, :] <= slot_ids[None, :, None]).astype(jnp.int32), axis=2)
    shuffles = jax.vmap(lambda one_key: jax.random.permutation(one_key, SEC_DEV))(jax.random.split(key_shuffle, devices))
    targets = jnp.take_along_axis(dest_sorted, shuffles, axis=1)
    flat_target = targets.reshape(-1)
    onehot = (flat_target[:, None] == jnp.arange(devices, dtype=jnp.int32)[None, :]).astype(jnp.int32)
    arrival = jnp.sum((jnp.cumsum(onehot, axis=0) - onehot) * onehot, axis=1)
    orders = jax.vmap(lambda one_key: jax.random.permutation(one_key, SEC_DEV))(jax.random.split(key_order, devices))
    return (flat_target * SEC_DEV + orders[flat_target, arrival]).astype(jnp.int32)


def environment(key):
    key_noise, key_diag = jax.random.split(key)
    raw_noise = jax.random.normal(key_noise, (WT, NSEC, B, B), jnp.float32)
    symmetric = (raw_noise + jnp.swapaxes(raw_noise, 2, 3)) * (1.0 / math.sqrt(2.0 * B))
    diag_shift = jax.random.uniform(key_diag, (WT, NSEC, 1, 1), jnp.float32, 0.5, 1.5)
    positions = jnp.arange(B, dtype=jnp.int32)
    identity = (positions[:, None] == positions[None, :]).astype(jnp.float32)
    return symmetric + diag_shift * identity[None, None, :, :]


def draw_left_environment(key, part):
    key = jax.random.fold_in(key, 53)
    return environment(key).astype(jnp.bfloat16)


def draw_right_environment(key, part):
    key = jax.random.fold_in(key, 59)
    return environment(key).astype(jnp.bfloat16)


def shard_levels(stream_key, dims, shards, least, high):
    factor_of = 1.0
    for position, parts in shards:
        draws = jax.random.uniform(jax.random.fold_in(jax.random.fold_in(stream_key, 6), position), (parts,), jnp.float32, least / len(shards), high / len(shards))
        factor_of = factor_of * jnp.repeat(jnp.exp(draws), dims[position] // parts).reshape((-1,) + (1,) * (len(dims) - 1 - position))
    return factor_of


def setup_inputs(seed: int = 0) -> dict:
    key_list = jax.random.split(jax.random.key(seed), 8)
    wavefunction = draw_wavefunction(jax.random.fold_in(key_list[7], 71), 0)
    left_size = draw_left_size(jax.random.fold_in(key_list[7], 71), 0)
    right_size = draw_right_size(jax.random.fold_in(key_list[7], 71), 0)
    right_sector = draw_right_sector(jax.random.fold_in(key_list[7], 71), 0)
    left_environment = draw_left_environment(jax.random.fold_in(key_list[7], 71), 0)
    right_environment = draw_right_environment(jax.random.fold_in(key_list[7], 71), 0)
    term_weights = jnp.clip(jax.random.uniform(key_list[6], (WT,), jnp.float32, -0.4, 0.4) * shard_levels(key_list[6], (WT,), ((0, 8),), -0.4, 0.0), -0.4, 0.4)
    return dict(wavefunction=wavefunction, left_size=left_size, right_size=right_size, right_sector=right_sector, left_environment=left_environment, right_environment=right_environment, term_weights=term_weights)


def live_blocks(left_size, right_size, right_sector):
    positions = jnp.arange(B, dtype=jnp.int32)
    partner_size = jnp.take(right_size, right_sector, axis=0)
    row_live = (positions[None, :] < left_size[:, None]).astype(jnp.float32)
    col_live = (positions[None, :] < partner_size[:, None]).astype(jnp.float32)
    return row_live[:, :, None] * col_live[:, None, :]

def apply_operator(vector, live_mask, left_environment, right_environment, right_sector, term_weights):
    rounded = vector.astype(jnp.bfloat16)

    def one_sector(inputs):
        sector_block, sector, partner = inputs
        left_terms = lax.dynamic_index_in_dim(left_environment, sector, 1, keepdims=False)
        right_terms = lax.dynamic_index_in_dim(right_environment, partner, 1, keepdims=False)
        half_term = jnp.einsum('wab,bc->wac', left_terms.astype(jnp.float32), sector_block.astype(jnp.float32))
        half_term = (term_weights[:, None, None] * half_term).astype(jnp.bfloat16)
        return jnp.einsum('wac,wdc->ad', half_term.astype(jnp.float32), right_terms.astype(jnp.float32))
    sectors = jnp.arange(NSEC, dtype=jnp.int32)
    applied = lax.map(one_sector, (rounded, sectors, right_sector.astype(jnp.int32)))
    return live_mask * applied

def reference(wavefunction, left_size, right_size, right_sector, left_environment, right_environment, term_weights):
    live_mask = live_blocks(left_size, right_size, right_sector)
    entries = float(NSEC * B * B)
    masked_start = live_mask * wavefunction.astype(jnp.float32)
    first_vector = masked_start / jnp.sqrt(jnp.sum(masked_start * masked_start) / entries + 1e-06)
    image_first = apply_operator(first_vector, live_mask, left_environment, right_environment, right_sector, term_weights)
    alpha_first = jnp.sum(first_vector * image_first) / entries
    lanczos_rest = image_first - alpha_first * first_vector
    beta_next = jnp.sqrt(jnp.sum(lanczos_rest * lanczos_rest) / entries + 1e-06)
    next_vector = lanczos_rest / beta_next
    image_next = apply_operator(next_vector, live_mask, left_environment, right_environment, right_sector, term_weights)
    alpha_next = jnp.sum(next_vector * image_next) / entries
    residual = image_next - alpha_next * next_vector - beta_next * first_vector
    coefficients = jnp.stack([alpha_first, beta_next, alpha_next])
    return (next_vector, residual, coefficients)
```

```python
import functools

import jax
import jax.numpy as jnp
from jax import lax
from jax.experimental import pallas as pl
from jax.experimental.pallas import tpu as pltpu
from jax.sharding import PartitionSpec as P

F32 = jnp.float32
BF16 = jnp.bfloat16
GROUPS = 2
UNROLL = 4


def flip(index, mask, size):
    out = index
    bit = 1
    while bit < size:
        if mask & bit:
            out = out + bit * (1 - 2 * ((index // bit) % 2))
        bit *= 2
    return out


def tree(values):
    values = list(values)
    while len(values) > 1:
        values = [values[i] + values[i + 1] for i in range(0, len(values), 2)]
    return values[0]


def fold(x):
    return jnp.sum(x.reshape(-1, 8, x.shape[-1]), axis=0)


def total(tile):
    return jnp.sum(jnp.sum(tile, axis=1, keepdims=True), axis=0, keepdims=True)


def kernel(
    devices, layers, capacity,
    wave, left_size, right_size, right_sector, left_env, right_env, weights,
    next_out, rest_out, coef_out,
    staged, held, place, first, half, mask, part, pair_in, z_out, z_in, gathered,
    norm_tiles, layer_tiles, sec_tiles, layer_tile2, sec_tile2,
    env_send, env_recv, local_sem, norm_send, norm_recv,
    pair_send, pair_recv, z_send, z_recv,
    gather_send, gather_recv, relay_send, relay_recv,
    layer_send, layer_recv, sec_send, sec_recv,
):
    blocks, width = wave.shape[0], wave.shape[1]
    terms = left_env.shape[0]
    depth = layers // 2
    rows = width // layers
    per_group = blocks // GROUPS
    entries = float(blocks * devices * width * width)
    sec = lax.axis_index("sec")
    mpo = lax.axis_index("mpo")
    z, core = mpo // 2, mpo % 2
    partner = 2 * z + 1 - core
    sec_peer = [flip(sec, k, devices) for k in range(devices)]
    mpo_peer = [flip(mpo, k, layers) for k in range(layers)]
    z_peer = [flip(z, k, depth) for k in range(depth)]
    order = list(range(depth - 1, 0, -1))
    started = []

    def send(src, dst, send_sem, recv_sem, to):
        copy = pltpu.make_async_remote_copy(
            src_ref=src, dst_ref=dst, send_sem=send_sem, recv_sem=recv_sem,
            device_id=to, device_id_type=pl.DeviceIdType.MESH,
        )
        copy.start()
        started.append(copy)
        return copy

    barrier = pltpu.get_barrier_semaphore()
    for k in range(1, devices):
        pl.semaphore_signal(barrier, inc=1, device_id=(sec_peer[k], mpo), device_id_type=pl.DeviceIdType.MESH)
    for k in range(1, layers):
        pl.semaphore_signal(barrier, inc=1, device_id=(sec, mpo_peer[k]), device_id_type=pl.DeviceIdType.MESH)

    own_start = (devices - 1) * capacity
    locals_ = []
    for t in range(terms):
        copy = pltpu.make_async_copy(right_env.at[t], held.at[t, pl.ds(own_start, blocks)], local_sem.at[t])
        copy.start()
        locals_.append(copy)

    def pack(k):
        base = sec_peer[k] * blocks

        def look(i, carry):
            count, found = carry[0], carry[1:]
            local = right_sector[base + i] - sec * blocks
            mine = (local >= 0) & (local < blocks)
            found = tuple(
                jnp.where(mine & (count == c), local, found[c]) for c in range(capacity)
            )
            return (count + mine.astype(jnp.int32),) + found

        carry = (jnp.int32(0),) * (capacity + 1)
        for i in range(blocks):
            carry = look(i, carry)
        for c in range(capacity):
            for t in range(terms):
                staged[k - 1, t, c] = right_env[t, carry[1 + c]]

    env_copies = []
    peer_order = list(range(devices - 1, 0, -1))
    for n, k in enumerate(peer_order):
        pack(k)
        if n == 0:
            pl.semaphore_wait(barrier, devices - 1 + layers - 1)
        for t in range(terms):
            env_copies.append(send(
                staged.at[k - 1, t], held.at[t, pl.ds((k - 1) * capacity, capacity)],
                env_send.at[k - 1, t], env_recv.at[k - 1, t], (sec_peer[k], mpo),
            ))

    counts = [jnp.int32(0)] * devices
    for i in range(blocks):
        sector = right_sector[sec * blocks + i]
        owner = sector // blocks
        at = own_start + sector - sec * blocks
        for k in range(1, devices):
            match = owner == sec_peer[k]
            at = jnp.where(match, (k - 1) * capacity + counts[k], at)
            counts[k] = counts[k] + match.astype(jnp.int32)
        place[i] = at

    row_ids = lax.broadcasted_iota(jnp.int32, (width, width), 0)
    col_ids = lax.broadcasted_iota(jnp.int32, (width, width), 1)
    slice_rows = lax.broadcasted_iota(jnp.int32, (rows, width), 0) + mpo * rows
    slice_cols = lax.broadcasted_iota(jnp.int32, (rows, width), 1)

    def masked_block(l, acc):
        live_rows = left_size[l]
        live_cols = right_size[right_sector[sec * blocks + l]]
        live = (row_ids < live_rows) & (col_ids < live_cols)
        block = jnp.where(live, wave[l].astype(F32), 0.0)
        first[l] = block
        live = (slice_rows < live_rows) & (slice_cols < live_cols)
        mask[l] = jnp.where(live, 1.0, 0.0)
        return acc + fold(block * block)

    norm_tiles[0] = lax.fori_loop(0, blocks, masked_block, jnp.zeros((8, width), F32))
    norm_copies = [
        send(norm_tiles.at[0], norm_tiles.at[k], norm_send.at[k], norm_recv.at[k], (sec_peer[k], mpo))
        for k in range(1, devices)
    ]
    for copy in norm_copies:
        copy.wait_recv()
    start_total = total(tree([norm_tiles[k] for k in range(devices)]))
    scale = 1.0 / jnp.sqrt(start_total * (1.0 / entries) + 1e-6)

    def left_block(l, v):
        stacked = jnp.concatenate([left_env[t, l] for t in range(terms)], axis=0)
        product = jnp.dot(stacked, v, preferred_element_type=F32)
        half[l] = jnp.concatenate(
            [(weights[t] * product[t * width:(t + 1) * width]).astype(BF16) for t in range(terms)], axis=1
        )

    def right_block(h, l):
        at = place[l]
        right = jnp.concatenate([held[t, at] for t in range(terms)], axis=1)
        out = lax.dot_general(half[l], right, (((1,), (1,)), ((), ())), preferred_element_type=F32)
        for m in range(layers):
            part[h, m % 2, m // 2, l] = out[m * rows:(m + 1) * rows]

    def loop_blocks(begin, end, body):
        def several(i, carry):
            for u in range(UNROLL):
                body(begin + i * UNROLL + u)
            return carry
        lax.fori_loop(0, (end - begin) // UNROLL, several, 0)

    def flat(g):
        return pl.ds(g * per_group * rows, per_group * rows)

    def pair_exchange(h, g):
        span = pl.ds(g * per_group, per_group)
        return {
            k: send(
                part.at[h, 1 - core, z_peer[k], span], pair_in.at[h, k, span],
                pair_send.at[h, g, k], pair_recv.at[h, g, k], (sec, partner),
            )
            for k in order + [0]
        }

    def z_exchange(h, g, pair_copies):
        span = pl.ds(g * per_group, per_group)
        copies = []
        for k in order:
            pair_copies[k].wait_recv()
            both = part[h, core, z_peer[k], span] + pair_in[h, k, span]
            z_out[h, k - 1, flat(g)] = both.reshape(per_group * rows, width).astype(BF16)
            copies.append(send(
                z_out.at[h, k - 1, flat(g)], z_in.at[h, k - 1, flat(g)],
                z_send.at[h, g, k - 1], z_recv.at[h, g, k - 1], (sec, 2 * z_peer[k] + core),
            ))
        pair_copies[0].wait_recv()
        return copies

    def image(h, z_copies):
        for copy in z_copies:
            copy.wait_recv()
        value = part[h, core, z] + pair_in[h, 0]
        for k in range(1, depth):
            value = value + z_in[h, k - 1].astype(F32).reshape(blocks, rows, width)
        return mask[...] * value

    def first_left(l):
        left_block(l, (first[l] * scale).astype(BF16))

    loop_blocks(0, blocks, first_left)
    for copy in locals_:
        copy.wait()
    for copy in env_copies:
        copy.wait_recv()
    pairs, z_copies = {}, []
    for g in range(GROUPS):
        loop_blocks(g * per_group, (g + 1) * per_group, functools.partial(right_block, 0))
        pairs[g] = pair_exchange(0, g)
        if g > 0:
            z_copies += z_exchange(0, g - 1, pairs[g - 1])
    z_copies += z_exchange(0, GROUPS - 1, pairs[GROUPS - 1])
    first_slice = first[:, pl.ds(pl.multiple_of(mpo * rows, rows), rows), :] * scale
    image_first = image(0, z_copies)

    inner = fold(first_slice * image_first)
    square = fold(first_slice * first_slice)
    lean = jnp.where(square > 1e-30, inner / jnp.where(square > 1e-30, square, 1.0), 0.0)
    away = image_first - lean[None, :, :] * first_slice if rows == 8 else (
        image_first - jnp.concatenate([lean] * (rows // 8), axis=0)[None] * first_slice
    )
    layer_tiles[0, 0] = inner
    layer_tiles[0, 1] = square
    layer_tiles[0, 2] = fold(away * away)
    layer_tiles[0, 3] = lean
    copies = [
        send(layer_tiles.at[0], layer_tiles.at[k], layer_send.at[0, k], layer_recv.at[0, k], (sec, mpo_peer[k]))
        for k in range(1, layers)
    ]
    for copy in copies:
        copy.wait_recv()

    def moved(a, inner, square, spread, lean):
        d = a - lean
        return spread - 2.0 * d * (inner - lean * square) + d * square * d

    inner = tree([layer_tiles[k, 0] for k in range(layers)])
    square = tree([layer_tiles[k, 1] for k in range(layers)])
    lean = jnp.where(square > 1e-30, inner / jnp.where(square > 1e-30, square, 1.0), 0.0)
    spread = tree([
        moved(lean, layer_tiles[k, 0], layer_tiles[k, 1], layer_tiles[k, 2], layer_tiles[k, 3])
        for k in range(layers)
    ])
    sec_tiles[0, 0] = inner
    sec_tiles[0, 1] = square
    sec_tiles[0, 2] = spread
    sec_tiles[0, 3] = lean
    copies = [
        send(sec_tiles.at[0], sec_tiles.at[k], sec_send.at[0, k], sec_recv.at[0, k], (sec_peer[k], mpo))
        for k in range(1, devices)
    ]
    for copy in copies:
        copy.wait_recv()
    alpha_first = total(tree([sec_tiles[k, 0] for k in range(devices)])) * (1.0 / entries)
    rest_total = total(tree([
        moved(alpha_first, sec_tiles[k, 0], sec_tiles[k, 1], sec_tiles[k, 2], sec_tiles[k, 3])
        for k in range(devices)
    ]))
    beta = jnp.sqrt(rest_total * (1.0 / entries) + 1e-6)
    next_slice = (image_first - alpha_first[None] * first_slice) / beta[None]

    gathered[mpo] = next_slice.reshape(blocks * rows, width).astype(BF16)
    direct, relayed = {}, {}
    for g in range(GROUPS):
        for k in order:
            direct[g, k] = send(
                gathered.at[mpo, flat(g)], gathered.at[mpo, flat(g)],
                gather_send.at[g, k], gather_recv.at[g, k], (sec, 2 * z_peer[k] + core),
            )
        relayed[g, 0] = send(
            gathered.at[mpo, flat(g)], gathered.at[mpo, flat(g)],
            relay_send.at[g, 0], relay_recv.at[g, 0], (sec, partner),
        )
    next_out[...] = next_slice

    def next_block(l):
        if rows % 16 == 0:
            pieces = [gathered[m, pl.ds(pl.multiple_of(l * rows, rows), rows)] for m in range(layers)]
            return jnp.concatenate(pieces, axis=0)
        pieces = [
            gathered[m, pl.ds((l * rows) // 16 * 16, 16)].astype(F32)[(l * rows) % 16:(l * rows) % 16 + rows]
            for m in range(layers)
        ]
        return jnp.concatenate(pieces, axis=0).astype(BF16)

    def second_block(l):
        left_block(l, next_block(l))

    pairs, z_copies = {}, []
    for g in range(GROUPS):
        for k in reversed(order):
            direct[g, k].wait_recv()
            from_there = 2 * z_peer[k] + core
            relayed[g, k] = send(
                gathered.at[from_there, flat(g)], gathered.at[from_there, flat(g)],
                relay_send.at[g, k], relay_recv.at[g, k], (sec, partner),
            )
        for k in [0] + order[::-1]:
            relayed[g, k].wait_recv()
        begin, end = g * per_group, (g + 1) * per_group
        if rows % 16 == 0:
            loop_blocks(begin, end, second_block)
        else:
            for l in range(begin, end):
                second_block(l)
        loop_blocks(begin, end, functools.partial(right_block, 1))
        pairs[g] = pair_exchange(1, g)
        if g > 0:
            z_copies += z_exchange(1, g - 1, pairs[g - 1])
    z_copies += z_exchange(1, GROUPS - 1, pairs[GROUPS - 1])
    image_next = image(1, z_copies)
    next_slice = next_out[...]

    layer_tile2[0] = fold(next_slice * image_next)
    copies = [
        send(layer_tile2.at[0], layer_tile2.at[k], layer_send.at[1, k], layer_recv.at[1, k], (sec, mpo_peer[k]))
        for k in range(1, layers)
    ]
    for copy in copies:
        copy.wait_recv()
    sec_tile2[0] = tree([layer_tile2[k] for k in range(layers)])
    copies = [
        send(sec_tile2.at[0], sec_tile2.at[k], sec_send.at[1, k], sec_recv.at[1, k], (sec_peer[k], mpo))
        for k in range(1, devices)
    ]
    for copy in copies:
        copy.wait_recv()
    alpha_next = total(tree([sec_tile2[k] for k in range(devices)])) * (1.0 / entries)
    first_slice = first[:, pl.ds(pl.multiple_of(mpo * rows, rows), rows), :] * scale
    rest_out[...] = image_next - alpha_next[None] * next_slice - beta[None] * first_slice
    coef_out[0] = jnp.max(alpha_first)
    coef_out[1] = jnp.max(beta)
    coef_out[2] = jnp.max(alpha_next)
    for copy in started:
        copy.wait_send()


def shards(wavefunction, left_size, right_size, right_sector, left_environment, right_environment, term_weights):
    blocks, width = wavefunction.shape[0], wavefunction.shape[1]
    terms = left_environment.shape[0]
    devices = lax.axis_size("sec")
    layers = lax.axis_size("mpo")
    depth = layers // 2
    rows = width // layers
    average = blocks // devices
    capacity = average + max(1, average // 2)
    dma = pltpu.SemaphoreType.DMA
    vmem = pl.BlockSpec(memory_space=pltpu.VMEM)
    smem = pl.BlockSpec(memory_space=pltpu.SMEM)
    return pl.pallas_call(
        functools.partial(kernel, devices, layers, capacity),
        out_shape=(
            jax.ShapeDtypeStruct((blocks, rows, width), F32),
            jax.ShapeDtypeStruct((blocks, rows, width), F32),
            jax.ShapeDtypeStruct((3,), F32),
        ),
        in_specs=[vmem, smem, smem, smem, vmem, vmem, smem],
        out_specs=(vmem, vmem, smem),
        scratch_shapes=[
            pltpu.VMEM((devices - 1, terms, capacity, width, width), BF16),
            pltpu.VMEM((terms, (devices - 1) * capacity + blocks, width, width), BF16),
            pltpu.SMEM((blocks,), jnp.int32),
            pltpu.VMEM((blocks, width, width), F32),
            pltpu.VMEM((blocks, width, terms * width), BF16),
            pltpu.VMEM((blocks, rows, width), F32),
            pltpu.VMEM((2, 2, depth, blocks, rows, width), F32),
            pltpu.VMEM((2, depth, blocks, rows, width), F32),
            pltpu.VMEM((2, depth - 1, blocks * rows, width), BF16),
            pltpu.VMEM((2, depth - 1, blocks * rows, width), BF16),
            pltpu.VMEM((layers, blocks * rows, width), BF16),
            pltpu.VMEM((devices, 8, width), F32),
            pltpu.VMEM((layers, 4, 8, width), F32),
            pltpu.VMEM((devices, 4, 8, width), F32),
            pltpu.VMEM((layers, 8, width), F32),
            pltpu.VMEM((devices, 8, width), F32),
            dma((devices - 1, terms)), dma((devices - 1, terms)), dma((terms,)),
            dma((devices,)), dma((devices,)),
            dma((2, GROUPS, depth)), dma((2, GROUPS, depth)),
            dma((2, GROUPS, depth)), dma((2, GROUPS, depth)),
            dma((GROUPS, depth)), dma((GROUPS, depth)),
            dma((GROUPS, depth)), dma((GROUPS, depth)),
            dma((2, layers)), dma((2, layers)),
            dma((2, devices)), dma((2, devices)),
        ],
        compiler_params=pltpu.CompilerParams(
            collective_id=0, has_side_effects=True, vmem_limit_bytes=40 * 1024 * 1024
        ),
    )(wavefunction, left_size, right_size, right_sector, left_environment, right_environment, term_weights)


def solution(mesh):
    placed = (
        P("sec", None, None),
        P("sec"),
        P(),
        P(),
        P("mpo", "sec", None, None),
        P("mpo", "sec", None, None),
        P("mpo"),
    )
    return jax.shard_map(
        shards,
        mesh=mesh,
        in_specs=placed,
        out_specs=(P("sec", "mpo", None), P("sec", "mpo", None), P()),
        check_vma=False,
    )
```

```python
import functools

import jax
import jax.numpy as jnp
from jax import lax
from jax.experimental import pallas as pl
from jax.experimental.pallas import tpu as pltpu
from jax.sharding import PartitionSpec as P

F32 = jnp.float32
BF16 = jnp.bfloat16
GROUPS = 2
UNROLL = 4


def flip(index, mask, size):
    out = index
    bit = 1
    while bit < size:
        if mask & bit:
            out = out + bit * (1 - 2 * ((index // bit) % 2))
        bit *= 2
    return out


def tree(values):
    values = list(values)
    while len(values) > 1:
        values = [values[i] + values[i + 1] for i in range(0, len(values), 2)]
    return values[0]


def fold(x):
    return jnp.sum(x.reshape(-1, 8, x.shape[-1]), axis=0)


def total(tile):
    return jnp.sum(jnp.sum(tile, axis=1, keepdims=True), axis=0, keepdims=True)


def kernel(
    devices, layers, capacity,
    wave_hbm, left_size_hbm, right_size_hbm, right_sector_hbm, left_hbm, right_hbm, weights_hbm,
    next_out, rest_out, coef_out,
    wave, left_size, right_size, right_sector, left_env, right_env, weights,
    staged, held, place, source, valid, first, half, mask,
    part1, pair_in1, z_out1, z_in1, part2, pair_in2, z_out2, z_in2,
    slot_image, rest, gathered,
    norm_tiles, layer1, sec1, layer2, sec2, layer3, sec3,
    load_sem, env_send, env_recv, norm_send, norm_recv,
    pair_send1, pair_recv1, z_send1, z_recv1, pair_send2, pair_recv2, z_send2, z_recv2,
    gather_send, gather_recv, relay_send, relay_recv,
    layer_send, layer_recv, sec_send, sec_recv,
):
    blocks, width = wave.shape[0], wave.shape[1]
    terms = left_env.shape[0]
    depth = layers // 2
    rows = width // layers
    per_group = blocks // GROUPS
    entries = float(blocks * devices * width * width)
    sec = lax.axis_index("sec")
    mpo = lax.axis_index("mpo")
    z, core = mpo // 2, mpo % 2
    partner = 2 * z + 1 - core
    sec_peer = [flip(sec, k, devices) for k in range(devices)]
    mpo_peer = [flip(mpo, k, layers) for k in range(layers)]
    z_peer = [flip(z, k, depth) for k in range(depth)]
    order = list(range(depth - 1, 0, -1))
    started = []

    def send(src, dst, send_sem, recv_sem, to):
        copy = pltpu.make_async_remote_copy(
            src_ref=src, dst_ref=dst, send_sem=send_sem, recv_sem=recv_sem,
            device_id=to, device_id_type=pl.DeviceIdType.MESH,
        )
        copy.start()
        started.append(copy)
        return copy

    loads = []
    pairs_of_refs = (
        (left_size_hbm, left_size), (right_size_hbm, right_size), (right_sector_hbm, right_sector),
        (weights_hbm, weights), (wave_hbm, wave), (right_hbm, right_env), (left_hbm, left_env),
    )
    for n, (src, dst) in enumerate(pairs_of_refs):
        copy = pltpu.make_async_copy(src, dst, load_sem.at[n])
        copy.start()
        loads.append(copy)

    barrier = pltpu.get_barrier_semaphore()
    for k in range(1, devices):
        pl.semaphore_signal(barrier, inc=1, device_id=(sec_peer[k], mpo), device_id_type=pl.DeviceIdType.MESH)
    for k in range(1, layers):
        pl.semaphore_signal(barrier, inc=1, device_id=(sec, mpo_peer[k]), device_id_type=pl.DeviceIdType.MESH)
    for copy in loads[:4]:
        copy.wait()

    def wanted(k):
        base = sec_peer[k] * blocks
        count = jnp.int32(0)
        found = [jnp.int32(0)] * capacity
        for i in range(blocks):
            local = right_sector[base + i] - sec * blocks
            mine = (local >= 0) & (local < blocks)
            found = [jnp.where(mine & (count == c), local, found[c]) for c in range(capacity)]
            count = count + mine.astype(jnp.int32)
        return found

    row_ids = lax.broadcasted_iota(jnp.int32, (width, width), 0)
    col_ids = lax.broadcasted_iota(jnp.int32, (width, width), 1)
    slice_rows = lax.broadcasted_iota(jnp.int32, (rows, width), 0) + mpo * rows
    slice_cols = lax.broadcasted_iota(jnp.int32, (rows, width), 1)

    def masked_block(l, acc):
        live_rows = left_size[l]
        live_cols = right_size[right_sector[sec * blocks + l]]
        live = (row_ids < live_rows) & (col_ids < live_cols)
        block = jnp.where(live, wave[l].astype(F32), 0.0)
        first[l] = block
        live = (slice_rows < live_rows) & (slice_cols < live_cols)
        mask[l] = jnp.where(live, 1.0, 0.0)
        return acc + fold(block * block)

    loads[4].wait()

    def masked_blocks(i, acc):
        for u in range(UNROLL):
            acc = masked_block(i * UNROLL + u, acc)
        return acc

    norm_tiles[0] = lax.fori_loop(0, blocks // UNROLL, masked_blocks, jnp.zeros((8, width), F32))
    pl.semaphore_wait(barrier, devices - 1 + layers - 1)
    norm_copies = [
        send(norm_tiles.at[0], norm_tiles.at[k], norm_send.at[k], norm_recv.at[k], (sec_peer[k], mpo))
        for k in range(1, devices)
    ]

    peers = sorted(range(1, devices), key=lambda k: (bin(k).count("1"), k))
    piece = 2 if capacity % 2 == 0 else capacity
    pieces = capacity // piece
    tables = {k: wanted(k) for k in peers}
    loads[5].wait()
    near = [k for k in peers if bin(k).count("1") == 1]
    far = [k for k in peers if bin(k).count("1") > 1]
    env_copies = {}
    for batch in (near, far):
        for p in range(pieces):
            for k in batch:
                for c in range(p * piece, (p + 1) * piece):
                    for t in range(terms):
                        staged[k - 1, c, t] = right_env[t, tables[k][c]]
                span = pl.ds(p * piece, piece)
                env_copies[k, p] = send(
                    staged.at[k - 1, span], held.at[k - 1, span],
                    env_send.at[k - 1, p], env_recv.at[k - 1, p], (sec_peer[k], mpo),
                )

    own = wanted(0)
    for k in range(devices):
        count = jnp.int32(0)
        found = [jnp.int32(0)] * capacity
        for i in range(blocks):
            sector = right_sector[sec * blocks + i] - sec_peer[k] * blocks
            match = (sector >= 0) & (sector < blocks)
            found = [jnp.where(match & (count == c), i, found[c]) for c in range(capacity)]
            at = k * capacity + jnp.minimum(count, capacity - 1)
            place[i] = at if k == 0 else jnp.where(match, at, place[i])
            count = count + match.astype(jnp.int32)
        for c in range(capacity):
            source[k * capacity + c] = found[c]
            valid[k * capacity + c] = (count > c).astype(jnp.int32)

    for copy in norm_copies:
        copy.wait_recv()
    start_total = total(tree([norm_tiles[k] for k in range(devices)]))
    scale = 1.0 / jnp.sqrt(start_total * (1.0 / entries) + 1e-6)

    def left_block(l, v):
        stacked = jnp.concatenate([left_env[t, l] for t in range(terms)], axis=0)
        product = jnp.dot(stacked, v, preferred_element_type=F32)
        half[l] = jnp.concatenate(
            [(weights[t] * product[t * width:(t + 1) * width]).astype(BF16) for t in range(terms)], axis=1
        )

    def right_product(left, right):
        return lax.dot_general(
            left, jnp.concatenate(right, axis=1), (((1,), (1,)), ((), ())), preferred_element_type=F32
        )

    def loop_blocks(begin, end, body, carry=None):
        def several(i, carry):
            for u in range(UNROLL):
                carry = body(begin + i * UNROLL + u, carry)
            return carry
        return lax.fori_loop(0, (end - begin) // UNROLL, several, carry)

    def put(part, at, out):
        for m in range(layers):
            part[m % 2, m // 2, at] = out[m * rows:(m + 1) * rows]

    class Sum:
        def __init__(self, part, pair_in, z_out, z_in, sems):
            self.part, self.pair_in, self.z_out, self.z_in = part, pair_in, z_out, z_in
            self.pair_send, self.pair_recv, self.z_send, self.z_recv = sems
            self.pairs, self.zs, self.spans = {}, {}, {}

        def begin(self, g, lo, count):
            span = pl.ds(lo, count)
            self.spans[g] = (lo, count)
            self.pairs[g] = {
                k: send(
                    self.part.at[1 - core, z_peer[k], span], self.pair_in.at[k, span],
                    self.pair_send.at[g, k], self.pair_recv.at[g, k], (sec, partner),
                )
                for k in order + [0]
            }

        def middle(self, g):
            lo, count = self.spans[g]
            span, flat = pl.ds(lo, count), pl.ds(lo * rows, count * rows)
            self.zs[g] = []
            for k in order:
                self.pairs[g][k].wait_recv()
                both = self.part[core, z_peer[k], span] + self.pair_in[k, span]
                self.z_out[k - 1, flat] = both.reshape(count * rows, width).astype(BF16)
                self.zs[g].append(send(
                    self.z_out.at[k - 1, flat], self.z_in.at[k - 1, flat],
                    self.z_send.at[g, k - 1], self.z_recv.at[g, k - 1], (sec, 2 * z_peer[k] + core),
                ))
            self.pairs[g][0].wait_recv()

        def end(self, g):
            lo, count = self.spans[g]
            span, flat = pl.ds(lo, count), pl.ds(lo * rows, count * rows)
            value = self.part[core, z, span] + self.pair_in[0, span]
            for copy in self.zs[g]:
                copy.wait_recv()
            for k in range(1, depth):
                value = value + self.z_in[k - 1, flat].astype(F32).reshape(count, rows, width)
            return value

    def spread(n, tiles_layer, tiles_sec, combine):
        copies = [
            send(tiles_layer.at[0], tiles_layer.at[k], layer_send.at[n, k], layer_recv.at[n, k], (sec, mpo_peer[k]))
            for k in range(1, layers)
        ]

        def onward():
            for copy in copies:
                copy.wait_recv()
            combine(tiles_layer, layers, tiles_sec)
            return [
                send(tiles_sec.at[0], tiles_sec.at[k], sec_send.at[n, k], sec_recv.at[n, k], (sec_peer[k], mpo))
                for k in range(1, devices)
            ]
        return onward

    loads[6].wait()

    def first_left(l, carry):
        left_block(l, (first[l] * scale).astype(BF16))
        return carry

    loop_blocks(0, blocks, first_left)
    sum1 = Sum(part1, pair_in1, z_out1, z_in1, (pair_send1, pair_recv1, z_send1, z_recv1))
    inner = jnp.zeros((8, width), F32)
    largest = jnp.zeros((8, width), F32)
    groups = [(0, 0, capacity)] + [(k, 0, capacity) for k in peers[:-1]]
    last = peers[-1]
    groups += [(last, 0, capacity - piece), (last, capacity - piece, capacity)] if pieces > 1 else [(last, 0, capacity)]
    for g, (k, lo, hi) in enumerate(groups):
        if k > 0:
            for p in range(lo // piece, hi // piece):
                env_copies[k, p].wait_recv()
        for c in range(lo, hi):
            at = k * capacity + c
            l = source[at]
            right = [right_env[t, own[c]] if k == 0 else held[k - 1, c, t] for t in range(terms)]
            out = right_product(half[l], right)
            put(part1, at, out)
            live = valid[at] > 0
            start = first[l]
            inner = inner + jnp.where(live, fold(start * out), 0.0)
            top = jnp.max(jnp.abs(out).reshape(-1, 8, width), axis=0)
            largest = jnp.maximum(largest, jnp.where(live, top, 0.0))
        sum1.begin(g, k * capacity + lo, hi - lo)
        if g > 0:
            sum1.middle(g - 1)

    def combine1(tiles, n, into):
        into[0, 0] = tree([tiles[k, 0] for k in range(n)])
        into[0, 1] = functools.reduce(jnp.maximum, [tiles[k, 1] for k in range(n)])

    layer1[0, 0] = inner * scale
    layer1[0, 1] = largest
    onward = spread(0, layer1, sec1, combine1)
    sum1.middle(len(groups) - 1)
    copies = onward()
    for g, (k, lo, hi) in enumerate(groups):
        slot_image[pl.ds(k * capacity + lo, hi - lo)] = sum1.end(g)
    for copy in copies:
        copy.wait_recv()
    alpha_first = total(tree([sec1[k, 0] for k in range(devices)])) * (1.0 / entries)
    peak = functools.reduce(jnp.maximum, [sec1[k, 1] for k in range(devices)])
    peak = jnp.max(jnp.max(peak, axis=1, keepdims=True), axis=0, keepdims=True)
    peak = jnp.maximum(peak, 1e-30)
    shrink = 1.0 / peak
    own_rows = pl.ds(pl.multiple_of(mpo * rows, rows), rows)
    for l in range(blocks):
        rest[l] = mask[l] * slot_image[place[l]] - alpha_first * (first[l, own_rows] * scale)
    value = rest[...]
    gathered[mpo] = (value * shrink[None]).reshape(blocks * rows, width).astype(BF16)

    def flat(g):
        return pl.ds(g * per_group * rows, per_group * rows)

    direct, relayed = {}, {}
    for g in range(GROUPS):
        for k in order:
            direct[g, k] = send(
                gathered.at[mpo, flat(g)], gathered.at[mpo, flat(g)],
                gather_send.at[g, k], gather_recv.at[g, k], (sec, 2 * z_peer[k] + core),
            )
        relayed[g, 0] = send(
            gathered.at[mpo, flat(g)], gathered.at[mpo, flat(g)],
            relay_send.at[g, 0], relay_recv.at[g, 0], (sec, partner),
        )

    def combine(tiles, n, into):
        into[0] = tree([tiles[k] for k in range(n)])

    layer2[0] = fold(value * value)
    beta_onward = spread(1, layer2, sec2, combine)

    def next_block(l):
        if rows % 16 == 0:
            pieces = [gathered[m, pl.ds(pl.multiple_of(l * rows, rows), rows)] for m in range(layers)]
            return jnp.concatenate(pieces, axis=0)
        pieces = [
            gathered[m, pl.ds((l * rows) // 16 * 16, 16)].astype(F32)[(l * rows) % 16:(l * rows) % 16 + rows]
            for m in range(layers)
        ]
        return jnp.concatenate(pieces, axis=0).astype(BF16)

    def second_left(l, carry):
        left_block(l, next_block(l))
        return carry

    def second_right(l, inner):
        at = place[l]
        right = [held[at // capacity, lax.rem(at, capacity), t] for t in range(terms)]
        out = right_product(half[l], right)
        put(part2, l, out)
        return inner + fold(next_block(l).astype(F32) * out)

    sum2 = Sum(part2, pair_in2, z_out2, z_in2, (pair_send2, pair_recv2, z_send2, z_recv2))
    for c in range(capacity):
        for t in range(terms):
            held[devices - 1, c, t] = right_env[t, own[c]]
    for l in range(blocks):
        at = place[l]
        place[l] = jnp.where(at < capacity, at + (devices - 1) * capacity, at - capacity)
    inner = jnp.zeros((8, width), F32)
    for g in range(GROUPS):
        for k in reversed(order):
            direct[g, k].wait_recv()
            from_there = 2 * z_peer[k] + core
            relayed[g, k] = send(
                gathered.at[from_there, flat(g)], gathered.at[from_there, flat(g)],
                relay_send.at[g, k], relay_recv.at[g, k], (sec, partner),
            )
        if g == 0:
            copies = beta_onward()
        for k in [0] + order[::-1]:
            relayed[g, k].wait_recv()
        begin, end = g * per_group, (g + 1) * per_group
        if rows % 16 == 0:
            loop_blocks(begin, end, second_left)
            inner = loop_blocks(begin, end, second_right, inner)
        else:
            for l in range(begin, end):
                second_left(l, None)
                inner = second_right(l, inner)
        sum2.begin(g, begin, per_group)
        if g > 0:
            sum2.middle(g - 1)
    layer3[0] = inner
    onward = spread(2, layer3, sec3, combine)
    sum2.middle(GROUPS - 1)
    for copy in copies:
        copy.wait_recv()
    rest_total = total(tree([sec2[k] for k in range(devices)]))
    beta = jnp.sqrt(rest_total * (1.0 / entries) + 1e-6)
    next_out[...] = rest[...] / beta[None]
    copies = onward()
    grow = peak / beta
    first_slice = first[:, own_rows, :] * scale
    for copy in copies:
        copy.wait_recv()
    alpha_next = total(tree([sec3[k] for k in range(devices)])) * (1.0 / entries) * grow * grow
    rest_out[...] = -alpha_next[None] * next_out[...] - beta[None] * first_slice
    coef_out[0] = jnp.max(alpha_first)
    coef_out[1] = jnp.max(beta)
    coef_out[2] = jnp.max(alpha_next)
    for g in range(GROUPS):
        span = pl.ds(g * per_group, per_group)
        rest_out[span] = rest_out[span] + mask[span] * sum2.end(g) * grow[None]
    for copy in started:
        copy.wait_send()


def shards(wavefunction, left_size, right_size, right_sector, left_environment, right_environment, term_weights):
    blocks, width = wavefunction.shape[0], wavefunction.shape[1]
    terms = left_environment.shape[0]
    devices = lax.axis_size("sec")
    layers = lax.axis_size("mpo")
    depth = layers // 2
    rows = width // layers
    average = blocks // devices
    capacity = average + max(1, average // 2)
    slots = devices * capacity
    dma = pltpu.SemaphoreType.DMA
    vmem = pl.BlockSpec(memory_space=pltpu.VMEM)
    smem = pl.BlockSpec(memory_space=pltpu.SMEM)
    hbm = pl.BlockSpec(memory_space=pl.ANY)

    def sum_scratch(count):
        return [
            pltpu.VMEM((2, depth, count, rows, width), F32),
            pltpu.VMEM((depth, count, rows, width), F32),
            pltpu.VMEM((depth - 1, count * rows, width), BF16),
            pltpu.VMEM((depth - 1, count * rows, width), BF16),
        ]

    many = devices + 1
    return pl.pallas_call(
        functools.partial(kernel, devices, layers, capacity),
        out_shape=(
            jax.ShapeDtypeStruct((blocks, rows, width), F32),
            jax.ShapeDtypeStruct((blocks, rows, width), F32),
            jax.ShapeDtypeStruct((3,), F32),
        ),
        in_specs=[hbm] * 7,
        out_specs=(vmem, vmem, smem),
        scratch_shapes=[
            pltpu.VMEM(wavefunction.shape, BF16),
            pltpu.SMEM(left_size.shape, jnp.int32),
            pltpu.SMEM(right_size.shape, jnp.int32),
            pltpu.SMEM(right_sector.shape, jnp.int32),
            pltpu.VMEM(left_environment.shape, BF16),
            pltpu.VMEM(right_environment.shape, BF16),
            pltpu.SMEM(term_weights.shape, F32),
            pltpu.VMEM((devices - 1, capacity, terms, width, width), BF16),
            pltpu.VMEM((devices, capacity, terms, width, width), BF16),
            pltpu.SMEM((blocks,), jnp.int32),
            pltpu.SMEM((slots,), jnp.int32),
            pltpu.SMEM((slots,), jnp.int32),
            pltpu.VMEM((blocks, width, width), F32),
            pltpu.VMEM((blocks, width, terms * width), BF16),
            pltpu.VMEM((blocks, rows, width), F32),
            *sum_scratch(slots),
            *sum_scratch(blocks),
            pltpu.VMEM((slots, rows, width), F32),
            pltpu.VMEM((blocks, rows, width), F32),
            pltpu.VMEM((layers, blocks * rows, width), BF16),
            pltpu.VMEM((devices, 8, width), F32),
            pltpu.VMEM((layers, 2, 8, width), F32),
            pltpu.VMEM((devices, 2, 8, width), F32),
            pltpu.VMEM((layers, 8, width), F32),
            pltpu.VMEM((devices, 8, width), F32),
            pltpu.VMEM((layers, 8, width), F32),
            pltpu.VMEM((devices, 8, width), F32),
            dma((7,)),
            dma((devices - 1, capacity)), dma((devices - 1, capacity)),
            dma((devices,)), dma((devices,)),
            dma((many, depth)), dma((many, depth)), dma((many, depth)), dma((many, depth)),
            dma((GROUPS, depth)), dma((GROUPS, depth)), dma((GROUPS, depth)), dma((GROUPS, depth)),
            dma((GROUPS, depth)), dma((GROUPS, depth)),
            dma((GROUPS, depth)), dma((GROUPS, depth)),
            dma((3, layers)), dma((3, layers)),
            dma((3, devices)), dma((3, devices)),
        ],
        compiler_params=pltpu.CompilerParams(
            collective_id=0, has_side_effects=True, vmem_limit_bytes=58 * 1024 * 1024
        ),
    )(wavefunction, left_size, right_size, right_sector, left_environment, right_environment, term_weights)


def solution(mesh):
    placed = (
        P("sec", None, None),
        P("sec"),
        P(),
        P(),
        P("mpo", "sec", None, None),
        P("mpo", "sec", None, None),
        P("mpo"),
    )
    return jax.shard_map(
        shards,
        mesh=mesh,
        in_specs=placed,
        out_specs=(P("sec", "mpo", None), P("sec", "mpo", None), P()),
        check_vma=False,
    )
```

```python
import functools

import jax
import jax.numpy as jnp
from jax import lax
from jax.experimental import pallas as pl
from jax.experimental.pallas import tpu as pltpu
from jax.sharding import PartitionSpec as P

F32 = jnp.float32
BF16 = jnp.bfloat16
UNROLL = 4


def flip(index, mask, size):
    out = index
    bit = 1
    while bit < size:
        if mask & bit:
            out = out + bit * (1 - 2 * ((index // bit) % 2))
        bit *= 2
    return out


def tree(values):
    values = list(values)
    while len(values) > 1:
        values = [values[i] + values[i + 1] for i in range(0, len(values), 2)]
    return values[0]


def fold(x):
    return jnp.sum(x.reshape(-1, 8, x.shape[-1]), axis=0)


def total(tile):
    return jnp.sum(jnp.sum(tile, axis=1, keepdims=True), axis=0, keepdims=True)


def kernel(
    devices, layers, capacity,
    wave_hbm, left_size_hbm, right_size_hbm, right_sector_hbm, left_hbm, right_hbm, weights_hbm,
    next_out, rest_out, coef_out,
    wave, left_size, right_size, right_sector, left_env, right_env, weights,
    staged, held, pool, place, slot_of, left_of, first, half, mask, first_rows,
    part1, pair_in1, z_out1, z_in1, part2, pair_in2, z_out2, z_in2,
    image, image2, rest, gathered,
    norm_tiles, layer0, layer1, sec1, layer2, sec2, layer3, sec3,
    load_sem, env_send, env_recv, norm_send, norm_recv,
    pair_send1, pair_recv1, z_send1, z_recv1, pair_send2, pair_recv2, z_send2, z_recv2,
    gather_send, gather_recv, relay_send, relay_recv,
    layer_send, layer_recv, sec_send, sec_recv,
):
    blocks, width = wave.shape[0], wave.shape[1]
    terms = left_env.shape[0]
    depth = layers // 2
    rows = width // layers
    entries = float(blocks * devices * width * width)
    sec = lax.axis_index("sec")
    mpo = lax.axis_index("mpo")
    z, core = mpo // 2, mpo % 2
    partner = 2 * z + 1 - core
    sec_peer = [flip(sec, k, devices) for k in range(devices)]
    mpo_peer = [flip(mpo, k, layers) for k in range(layers)]
    z_peer = [flip(z, k, depth) for k in range(depth)]
    order = list(range(depth - 1, 0, -1))
    started = []

    def send(src, dst, send_sem, recv_sem, to):
        copy = pltpu.make_async_remote_copy(
            src_ref=src, dst_ref=dst, send_sem=send_sem, recv_sem=recv_sem,
            device_id=to, device_id_type=pl.DeviceIdType.MESH,
        )
        copy.start()
        started.append(copy)
        return copy

    loads = []
    pairs_of_refs = (
        (left_size_hbm, left_size), (right_size_hbm, right_size), (right_sector_hbm, right_sector),
        (weights_hbm, weights), (wave_hbm, wave), (right_hbm, right_env), (left_hbm, left_env),
    )
    for n, (src, dst) in enumerate(pairs_of_refs):
        copy = pltpu.make_async_copy(src, dst, load_sem.at[n])
        copy.start()
        loads.append(copy)

    barrier = pltpu.get_barrier_semaphore()
    for k in range(1, devices):
        pl.semaphore_signal(barrier, inc=1, device_id=(sec_peer[k], mpo), device_id_type=pl.DeviceIdType.MESH)
    for k in range(1, layers):
        pl.semaphore_signal(barrier, inc=1, device_id=(sec, mpo_peer[k]), device_id_type=pl.DeviceIdType.MESH)
    for c in range(capacity, devices * capacity):
        pool[c] = jnp.zeros(pool.shape[1:], BF16)
    for copy in loads[:4]:
        copy.wait()

    def wanted(k):
        base = sec_peer[k] * blocks
        count = jnp.int32(0)
        found = [jnp.int32(0)] * capacity
        for i in range(blocks):
            local = right_sector[base + i] - sec * blocks
            mine = (local >= 0) & (local < blocks)
            found = [jnp.where(mine & (count == c), local, found[c]) for c in range(capacity)]
            count = count + mine.astype(jnp.int32)
        return found

    row_ids = lax.broadcasted_iota(jnp.int32, (width, width), 0)
    col_ids = lax.broadcasted_iota(jnp.int32, (width, width), 1)
    slice_rows = lax.broadcasted_iota(jnp.int32, (rows, width), 0) + mpo * rows
    slice_cols = lax.broadcasted_iota(jnp.int32, (rows, width), 1)

    def masked_block(l, acc):
        live_rows = left_size[l]
        live_cols = right_size[right_sector[sec * blocks + l]]
        live = (row_ids < live_rows) & (col_ids < live_cols)
        block = jnp.where(live, wave[l].astype(F32), 0.0)
        first[l] = block
        live = (slice_rows < live_rows) & (slice_cols < live_cols)
        mask[l] = jnp.where(live, 1.0, 0.0)
        return acc + fold(block * block)

    loads[4].wait()

    def masked_blocks(i, acc):
        for u in range(UNROLL):
            acc = masked_block(i * UNROLL + u, acc)
        return acc

    norm_tiles[0, 0] = lax.fori_loop(0, blocks // UNROLL, masked_blocks, jnp.zeros((8, width), F32))
    loads[5].wait()

    def top(x):
        return jnp.max(jnp.abs(x).astype(F32).reshape(-1, 8, x.shape[-1]), axis=0)

    def largest_right(l, acc):
        for t in range(terms):
            acc = jnp.maximum(acc, top(right_env[t, l]))
        return acc

    norm_tiles[0, 1] = lax.fori_loop(0, blocks, largest_right, jnp.zeros((8, width), F32))
    pl.semaphore_wait(barrier, devices - 1 + layers - 1)
    norm_copies = [
        send(norm_tiles.at[0], norm_tiles.at[k], norm_send.at[k], norm_recv.at[k], (sec_peer[k], mpo))
        for k in range(1, devices)
    ]

    peers = sorted(range(1, devices), key=lambda k: (bin(k).count("1"), k))
    piece = 2 if capacity % 2 == 0 else capacity
    pieces = capacity // piece
    tables = {k: wanted(k) for k in peers}
    near = [k for k in peers if bin(k).count("1") == 1]
    far = [k for k in peers if bin(k).count("1") > 1]
    env_copies = {}
    for batch in (near, far):
        for p in range(pieces):
            for k in batch:
                for c in range(p * piece, (p + 1) * piece):
                    for t in range(terms):
                        staged[k - 1, c, t] = right_env[t, tables[k][c]]
                span = pl.ds(p * piece, piece)
                env_copies[k, p] = send(
                    staged.at[k - 1, span], held.at[k - 1, span],
                    env_send.at[k - 1, p], env_recv.at[k - 1, p], (sec_peer[k], mpo),
                )

    own = wanted(0)

    def arrival(k, c):
        if k == 0:
            return c
        batch, start = (near, capacity) if k in near else (far, capacity * (1 + len(near)))
        return start + (c // piece) * (len(batch) * piece) + batch.index(k) * piece + lax.rem(c, jnp.int32(piece))

    slots = [jnp.int32(0)] * blocks
    for k in range(devices):
        count = jnp.int32(0)
        for i in range(blocks):
            sector = right_sector[sec * blocks + i] - sec_peer[k] * blocks
            match = (sector >= 0) & (sector < blocks)
            slots[i] = jnp.where(match, arrival(k, jnp.minimum(count, capacity - 1)), slots[i])
            count = count + match.astype(jnp.int32)
    ranks = []
    for i in range(blocks):
        rank = jnp.int32(0)
        for j in range(blocks):
            if j != i:
                rank = rank + (slots[j] < slots[i]).astype(jnp.int32)
        ranks.append(rank)
        place[i] = rank
    for q in range(blocks):
        slot, left = jnp.int32(0), jnp.int32(0)
        for i in range(blocks):
            slot = jnp.where(ranks[i] == q, slots[i], slot)
            left = jnp.where(ranks[i] == q, i, left)
        slot_of[q] = slot
        left_of[q] = left
    for c in range(capacity):
        for t in range(terms):
            pool[c, t] = right_env[t, own[c]]

    for copy in norm_copies:
        copy.wait_recv()
    start_total = total(tree([norm_tiles[k, 0] for k in range(devices)]))
    scale = 1.0 / jnp.sqrt(start_total * (1.0 / entries) + 1e-6)

    def left_block(l, v):
        stacked = jnp.concatenate([left_env[t, l] for t in range(terms)], axis=0)
        product = jnp.dot(stacked, v, preferred_element_type=F32)
        half[l] = jnp.concatenate(
            [(weights[t] * product[t * width:(t + 1) * width]).astype(BF16) for t in range(terms)], axis=1
        )

    def right_product(left, right):
        return lax.dot_general(
            left, jnp.concatenate(right, axis=1), (((1,), (1,)), ((), ())), preferred_element_type=F32
        )

    def loop_blocks(begin, end, body, carry=None):
        def several(i, carry):
            for u in range(UNROLL):
                carry = body(begin + i * UNROLL + u, carry)
            return carry
        return lax.fori_loop(0, (end - begin) // UNROLL, several, carry)

    def put(part, at, out):
        for m in range(layers):
            part[m % 2, m // 2, at] = out[m * rows:(m + 1) * rows]

    class Sum:
        def __init__(self, part, pair_in, z_out, z_in, sems):
            self.part, self.pair_in, self.z_out, self.z_in = part, pair_in, z_out, z_in
            self.pair_send, self.pair_recv, self.z_send, self.z_recv = sems
            self.pairs, self.zs, self.spans = {}, {}, {}

        def begin(self, g, lo, count):
            span = pl.ds(lo, count)
            self.spans[g] = (lo, count)
            self.pairs[g] = {
                k: send(
                    self.part.at[1 - core, z_peer[k], span], self.pair_in.at[k, span],
                    self.pair_send.at[g, k], self.pair_recv.at[g, k], (sec, partner),
                )
                for k in order + [0]
            }

        def middle(self, g):
            lo, count = self.spans[g]
            span, flat = pl.ds(lo, count), pl.ds(lo * rows, count * rows)
            self.zs[g] = []
            for k in order:
                self.pairs[g][k].wait_recv()
                both = self.part[core, z_peer[k], span] + self.pair_in[k, span]
                self.z_out[k - 1, flat] = both.reshape(count * rows, width).astype(BF16)
                self.zs[g].append(send(
                    self.z_out.at[k - 1, flat], self.z_in.at[k - 1, flat],
                    self.z_send.at[g, k - 1], self.z_recv.at[g, k - 1], (sec, 2 * z_peer[k] + core),
                ))
            self.pairs[g][0].wait_recv()

        def end(self, g):
            lo, count = self.spans[g]
            span, flat = pl.ds(lo, count), pl.ds(lo * rows, count * rows)
            value = self.part[core, z, span] + self.pair_in[0, span]
            for copy in self.zs[g]:
                copy.wait_recv()
            for k in range(1, depth):
                value = value + self.z_in[k - 1, flat].astype(F32).reshape(count, rows, width)
            return value

    def spread(n, tiles_layer, tiles_sec, combine):
        copies = [
            send(tiles_layer.at[0], tiles_layer.at[k], layer_send.at[n, k], layer_recv.at[n, k], (sec, mpo_peer[k]))
            for k in range(1, layers)
        ]

        def onward():
            for copy in copies:
                copy.wait_recv()
            combine(tiles_layer, layers, tiles_sec)
            return [
                send(tiles_sec.at[0], tiles_sec.at[k], sec_send.at[n, k], sec_recv.at[n, k], (sec_peer[k], mpo))
                for k in range(1, devices)
            ]
        return onward

    loads[6].wait()

    def first_left(l, acc):
        left_block(l, (first[l] * scale).astype(BF16))
        return jnp.maximum(acc, top(half[l][:, :width])) if terms == 1 else jnp.maximum(
            acc, functools.reduce(jnp.maximum, [top(half[l][:, t * width:(t + 1) * width]) for t in range(terms)])
        )

    layer0[0, 0] = loop_blocks(0, blocks, first_left, jnp.zeros((8, width), F32))
    layer0[0, 1] = functools.reduce(jnp.maximum, [norm_tiles[k, 1] for k in range(devices)])
    scale_copies = [
        send(layer0.at[0], layer0.at[k], layer_send.at[3, k], layer_recv.at[3, k], (sec, mpo_peer[k]))
        for k in range(1, layers)
    ]
    own_rows = pl.ds(pl.multiple_of(mpo * rows, rows), rows)
    for q in range(blocks):
        first_rows[q] = first[left_of[q], own_rows] * scale

    batches, taken, begun = [], 0, 0
    stages = [[(k, p) for k in near] for p in range(pieces)] + [[(k, p) for k in far] for p in range(pieces)]
    missing = (devices - 1) * capacity
    waiting = []
    for n, stage in enumerate(stages):
        waiting += stage
        missing -= len(stage) * piece
        ready = max(0, blocks - missing) // 2 * 2
        final = n == len(stages) - 1
        if final or ready - taken >= 4:
            batches.append((taken, ready - taken, waiting))
            taken, waiting = ready, []
    sum1 = Sum(part1, pair_in1, z_out1, z_in1, (pair_send1, pair_recv1, z_send1, z_recv1))
    sum2 = Sum(part2, pair_in2, z_out2, z_in2, (pair_send2, pair_recv2, z_send2, z_recv2))
    sums = {"inner": jnp.zeros((8, width), F32), "own": jnp.zeros((8, width), F32), "cross": jnp.zeros((8, width), F32)}
    direct, relayed, peak = {}, {}, []

    def flat(b):
        lo, count, _ = batches[b]
        return pl.ds(lo * rows, count * rows)

    def step_right(b):
        lo, count, pieces_there = batches[b]
        for k, p in pieces_there:
            env_copies[k, p].wait_recv()
            for c in range(p * piece, (p + 1) * piece):
                batch, start = (near, capacity) if k in near else (far, capacity * (1 + len(near)))
                at = start + (c // piece) * (len(batch) * piece) + batch.index(k) * piece + c % piece
                for t in range(terms):
                    pool[at, t] = held[k - 1, c, t]
        for q in range(lo, lo + count):
            l, at = left_of[q], slot_of[q]
            out = right_product(half[l], [pool[at, t] for t in range(terms)])
            put(part1, q, out)
            sums["inner"] = sums["inner"] + fold(first[l] * out)
        sum1.begin(b, lo, count)

    def step_middle(b):
        sum1.middle(b)

    def step_gather(b):
        lo, count, _ = batches[b]
        if not peak:
            for copy in scale_copies:
                copy.wait_recv()
            for n in range(2):
                tile = functools.reduce(jnp.maximum, [layer0[k, n] for k in range(layers)])
                tile = jnp.max(jnp.max(tile, axis=1, keepdims=True), axis=0, keepdims=True)
                peak.append(jnp.maximum(tile, 1e-18))
        live = jnp.stack([mask[left_of[q]] for q in range(lo, lo + count)])
        value = sum1.end(b) * live
        image[pl.ds(lo, count)] = value
        small = value * (1.0 / peak[0])[None] * (1.0 / peak[1])[None]
        gathered[mpo, flat(b)] = small.reshape(count * rows, width).astype(BF16)
        here = gathered.at[mpo, flat(b)]
        for k in order:
            direct[b, k] = send(here, here, gather_send.at[b, k], gather_recv.at[b, k], (sec, 2 * z_peer[k] + core))
        relayed[b, 0] = send(here, here, relay_send.at[b, 0], relay_recv.at[b, 0], (sec, partner))

    def step_relay(b):
        for k in reversed(order):
            direct[b, k].wait_recv()
            here = gathered.at[2 * z_peer[k] + core, flat(b)]
            relayed[b, k] = send(here, here, relay_send.at[b, k], relay_recv.at[b, k], (sec, partner))

    def image_block(q):
        if rows % 16 == 0:
            return jnp.concatenate([gathered[m, pl.ds(q * rows, rows)] for m in range(layers)], axis=0)
        low = (q * rows) // 16 * 16
        cut = q * rows - low
        blocks16 = [gathered[m, pl.ds(low, 16)].astype(F32)[cut:cut + rows] for m in range(layers)]
        return jnp.concatenate(blocks16, axis=0).astype(BF16)

    def step_second(b):
        lo, count, _ = batches[b]
        for k in [0] + order[::-1]:
            relayed[b, k].wait_recv()
        for q in range(lo, lo + count):
            l, at = left_of[q], slot_of[q]
            v = image_block(q)
            stacked = jnp.concatenate([left_env[t, l] for t in range(terms)], axis=0)
            product = jnp.dot(stacked, v, preferred_element_type=F32)
            left = jnp.concatenate(
                [(weights[t] * product[t * width:(t + 1) * width]).astype(BF16) for t in range(terms)], axis=1
            )
            out = right_product(left, [pool[at, t] for t in range(terms)])
            put(part2, q, out)
            sums["own"] = sums["own"] + fold(v.astype(F32) * out)
            sums["cross"] = sums["cross"] + fold(first[l] * out)
        sum2.begin(b, lo, count)

    def step_last(b):
        sum2.middle(b)

    def combine(tiles, n, into):
        for c in range(into.shape[1]):
            into[0, c] = tree([tiles[k, c] for k in range(n)])

    def mean(tiles, c):
        return total(tree([tiles[k, c] for k in range(devices)])) * (1.0 / entries)

    steps = (step_right, step_middle, step_gather, step_relay, step_second, step_last)
    offsets = (0.0, 1.5, 3.5, 5.5, 7.0, 8.5)
    starts = [3.0 * b if b < len(batches) // 2 else 3.0 * b + 2.0 for b in range(len(batches))]
    plan = sorted(
        (starts[b] + offsets[i], b, i) for b in range(len(batches)) for i in range(len(steps))
    )
    end = len(batches) - 1
    alpha_first = rest_copies = rest_onward = alpha_copies = None
    for _, b, i in plan:
        steps[i](b)
        if b < end:
            continue
        if i == 0:
            layer1[0, 0] = sums["inner"] * scale
            onward = spread(0, layer1, sec1, combine)
        if i == 1:
            alpha_copies = onward()
        if i == 2:
            for copy in alpha_copies:
                copy.wait_recv()
            alpha_first = total(tree([sec1[k, 0] for k in range(devices)])) * (1.0 / entries)
            value = image[...]
            away = value - alpha_first[None] * first_rows[...]
            rest[...] = away
            layer2[0, 0] = fold(away * away)
            layer2[0, 1] = fold(value * value)
            rest_onward = spread(1, layer2, sec2, combine)
        if i == 3:
            rest_copies = rest_onward()
        if i == 4:
            for copy in rest_copies:
                copy.wait_recv()
            beta = jnp.sqrt(mean(sec2, 0) + 1e-6)
            grow = peak[0] * (peak[1] / beta)
            layer3[0, 0] = sums["own"] * grow * grow
            layer3[0, 1] = sums["cross"] * scale * grow
            onward = spread(2, layer3, sec3, combine)
    image_square = mean(sec2, 1)
    rest[...] = rest[...] / beta[None]
    for l in range(blocks):
        next_out[l] = rest[place[l]]
    alpha_copies = onward()
    for b in range(len(batches)):
        lo, count, _ = batches[b]
        image2[pl.ds(lo, count)] = sum2.end(b)
    for copy in alpha_copies:
        copy.wait_recv()
    ratio = alpha_first / beta
    alpha_next = (
        mean(sec3, 0) - ratio * (image_square / beta) - ratio * mean(sec3, 1)
        + ratio * ratio * alpha_first
    )
    for l in range(blocks):
        q = place[l]
        applied = mask[l] * image2[q] * grow - ratio * image[q]
        rest_out[l] = applied - alpha_next * next_out[l] - beta * first_rows[q]
    coef_out[0] = jnp.max(alpha_first)
    coef_out[1] = jnp.max(beta)
    coef_out[2] = jnp.max(alpha_next)
    for copy in started:
        copy.wait_send()


def shards(wavefunction, left_size, right_size, right_sector, left_environment, right_environment, term_weights):
    blocks, width = wavefunction.shape[0], wavefunction.shape[1]
    terms = left_environment.shape[0]
    devices = lax.axis_size("sec")
    layers = lax.axis_size("mpo")
    depth = layers // 2
    rows = width // layers
    average = blocks // devices
    capacity = average + max(1, average // 2)
    slots = devices * capacity
    dma = pltpu.SemaphoreType.DMA
    vmem = pl.BlockSpec(memory_space=pltpu.VMEM)
    smem = pl.BlockSpec(memory_space=pltpu.SMEM)
    hbm = pl.BlockSpec(memory_space=pl.ANY)

    def sum_scratch(count):
        return [
            pltpu.VMEM((2, depth, count, rows, width), F32),
            pltpu.VMEM((depth, count, rows, width), F32),
            pltpu.VMEM((depth - 1, count * rows, width), BF16),
            pltpu.VMEM((depth - 1, count * rows, width), BF16),
        ]

    many = devices + 1
    return pl.pallas_call(
        functools.partial(kernel, devices, layers, capacity),
        out_shape=(
            jax.ShapeDtypeStruct((blocks, rows, width), F32),
            jax.ShapeDtypeStruct((blocks, rows, width), F32),
            jax.ShapeDtypeStruct((3,), F32),
        ),
        in_specs=[hbm] * 7,
        out_specs=(vmem, vmem, smem),
        scratch_shapes=[
            pltpu.VMEM(wavefunction.shape, BF16),
            pltpu.SMEM(left_size.shape, jnp.int32),
            pltpu.SMEM(right_size.shape, jnp.int32),
            pltpu.SMEM(right_sector.shape, jnp.int32),
            pltpu.VMEM(left_environment.shape, BF16),
            pltpu.VMEM(right_environment.shape, BF16),
            pltpu.SMEM(term_weights.shape, F32),
            pltpu.VMEM((devices - 1, capacity, terms, width, width), BF16),
            pltpu.VMEM((devices - 1, capacity, terms, width, width), BF16),
            pltpu.VMEM((slots, terms, width, width), BF16),
            pltpu.SMEM((blocks,), jnp.int32),
            pltpu.SMEM((blocks,), jnp.int32),
            pltpu.SMEM((blocks,), jnp.int32),
            pltpu.VMEM((blocks, width, width), F32),
            pltpu.VMEM((blocks, width, terms * width), BF16),
            pltpu.VMEM((blocks, rows, width), F32),
            pltpu.VMEM((blocks, rows, width), F32),
            *sum_scratch(blocks),
            *sum_scratch(blocks),
            pltpu.VMEM((blocks, rows, width), F32),
            pltpu.VMEM((blocks, rows, width), F32),
            pltpu.VMEM((blocks, rows, width), F32),
            pltpu.VMEM((layers, blocks * rows, width), BF16),
            pltpu.VMEM((devices, 2, 8, width), F32),
            pltpu.VMEM((layers, 2, 8, width), F32),
            pltpu.VMEM((layers, 1, 8, width), F32),
            pltpu.VMEM((devices, 1, 8, width), F32),
            pltpu.VMEM((layers, 2, 8, width), F32),
            pltpu.VMEM((devices, 2, 8, width), F32),
            pltpu.VMEM((layers, 2, 8, width), F32),
            pltpu.VMEM((devices, 2, 8, width), F32),
            dma((7,)),
            dma((devices - 1, capacity)), dma((devices - 1, capacity)),
            dma((devices,)), dma((devices,)),
            dma((many, depth)), dma((many, depth)), dma((many, depth)), dma((many, depth)),
            dma((many, depth)), dma((many, depth)), dma((many, depth)), dma((many, depth)),
            dma((many, depth)), dma((many, depth)),
            dma((many, depth)), dma((many, depth)),
            dma((4, layers)), dma((4, layers)),
            dma((3, devices)), dma((3, devices)),
        ],
        compiler_params=pltpu.CompilerParams(
            collective_id=0, has_side_effects=True, vmem_limit_bytes=58 * 1024 * 1024
        ),
    )(wavefunction, left_size, right_size, right_sector, left_environment, right_environment, term_weights)


def solution(mesh):
    placed = (
        P("sec", None, None),
        P("sec"),
        P(),
        P(),
        P("mpo", "sec", None, None),
        P("mpo", "sec", None, None),
        P("mpo"),
    )
    return jax.shard_map(
        shards,
        mesh=mesh,
        in_specs=placed,
        out_specs=(P("sec", "mpo", None), P("sec", "mpo", None), P()),
        check_vma=False,
    )
```
